128 devices in a mesh: segment: 2 (over x_lo), seq: 16 (over x_hi, y, core), head: 4 (over z).
Axes of the slice: x: 4 (x_hi: 2, x_lo: 2; x = x_hi * 2 + x_lo), y: 4, z: 4, core: 2. Of those that a mesh axis runs over, the one named last changes fastest.
Arguments:
- stream: bfloat16 [2, 2048, 4096], P(None, 'seq', 'head'), may hold values from -6 to 6
- in_gain: float32 [2, 4096], P('segment'), may hold values from 0.25 to 1.75
- w_qkv: bfloat16 [2, 4096, 4, 3, 512], P('segment', None, 'head'), may hold values from -0.09375 to 0.09375
- qk_gain: float32 [2, 4, 2, 512], P('segment', 'head'), may hold values from 0.25 to 1.75
- w_one: bfloat16 [2, 4, 512, 768], P('segment', 'head'), may hold values from -0.25 to 0.25
- w_three: bfloat16 [2, 4, 512, 768], P('segment', 'head'), may hold values from -0.25 to 0.25
- w_two: bfloat16 [2, 4, 768, 512], P('segment', 'head'), may hold values from -0.21875 to 0.21875
- token_rate: float32 [2, 2, 2048], P('segment', None, 'seq'), may hold values from 0.05 to 1
- out_gain: float32 [2, 4, 512], P('segment', 'head'), may hold values from 0.25 to 1.75
- w_out: bfloat16 [2, 4, 512, 4096], P('segment', 'head'), may hold values from -0.125 to 0.125
Outputs:
- sections_out: bfloat16 [2, 2, 2048, 4096], P('segment', None, 'seq', 'head')
The draws below stay inside these ranges and needn't reach their ends.
All inputs are finite; a program needn't handle non-finite values.
Results may differ from the reference program's by a relative error of at most 0.038.
Values may be sent and summed in bfloat16 or wider, within the bound.
No kernel may reach another device: no remote copies, remote signals or barrier semaphores. Data moves between devices by JAX's collectives and lax.ppermute only.
A program may use at most 128 MiB of HBM per device.

```python
import math
import jax
import jax.numpy as jnp
from jax import lax

DH = 512
FF = 768
HEADS = 4
DM = 4096
SECTIONS = 2
SPANS = 2
NS_STEPS = 2
TOKENS = 2048
N_SEQ = 16


def block_levels(stream_key, dims, split, least, high):
    gain = 1.0
    for axis_at, blocks in split:
        steps = jax.random.uniform(jax.random.fold_in(jax.random.fold_in(stream_key, 6), axis_at), (blocks,), jnp.float32, least / len(split), high / len(split))
        gain = gain * jnp.repeat(jnp.exp(steps), dims[axis_at] // blocks).reshape((-1,) + (1,) * (len(dims) - 1 - axis_at))
    return gain


def gaussian(own_key, shape, spread, limit, pieces=(), held_as=jnp.bfloat16):
    entries = jax.random.normal(own_key, shape, jnp.float32) * spread
    if len(pieces) > 0:
        entries = block_levels(own_key, shape, pieces, -0.22, 0.18) * entries
    return jnp.clip(entries, min=-limit, max=limit).astype(held_as)


def setup_inputs(seed: int = 0) -> dict:
    keys = jax.random.split(jax.random.key(seed), 11)
    stream = gaussian(keys[0], (SPANS, TOKENS, DM), 1.0, 6.0, ((1, 16), (2, 4)))
    in_gain = jnp.clip(1.0 + 0.15 * jax.random.normal(keys[1], (SECTIONS, DM), jnp.float32), 0.25, 1.75)
    w_qkv = gaussian(keys[2], (SECTIONS, DM, HEADS, 3, DH), DM ** -0.5, 0.09375, ((0, 2), (2, 4)))
    qk_gain = jnp.clip(1.0 + 0.15 * jax.random.normal(keys[3], (SECTIONS, HEADS, 2, DH), jnp.float32), 0.25, 1.75)
    w_one = gaussian(keys[4], (SECTIONS, HEADS, DH, FF), DH ** -0.5, 0.25, ((0, 2), (1, 4)))
    w_three = gaussian(keys[5], (SECTIONS, HEADS, DH, FF), DH ** -0.5, 0.25, ((0, 2), (1, 4)))
    w_two = gaussian(keys[6], (SECTIONS, HEADS, FF, DH), FF ** -0.5, 0.21875, ((0, 2), (1, 4)))
    token_rate = jnp.clip(jnp.exp(math.log(1.0) - 2.9957323 * jax.random.uniform(keys[7], (SECTIONS, SPANS, TOKENS), jnp.float32) ** block_levels(keys[7], (SECTIONS, SPANS, TOKENS), ((0, 2), (2, 16)), -0.2, 0.2)), 0.05, 1.0)
    out_gain = jnp.clip(1.0 + 0.15 * jax.random.normal(keys[8], (SECTIONS, HEADS, DH), jnp.float32), 0.25, 1.75)
    w_out = gaussian(keys[9], (SECTIONS, HEADS, DH, DM), (HEADS * DH) ** -0.5, 0.125, ((0, 2), (1, 4)))
    return dict(stream=stream, in_gain=in_gain, w_qkv=w_qkv, qk_gain=qk_gain, w_one=w_one, w_three=w_three, w_two=w_two, token_rate=token_rate, out_gain=out_gain, w_out=w_out)


ns_first = 3.4445
ns_second = -4.775
ns_third = 2.0315
update_step = 1.0
norm_eps = 1e-06
grad_eps = 1e-07

def rms_scale(values):
    return values * lax.rsqrt(lax.optimization_barrier(jnp.mean(values * values, axis=-1, keepdims=True)) + norm_eps)

def orthogonalize(gradient):
    current = (gradient / (jnp.sqrt(jnp.sum(gradient * gradient)) + grad_eps)).astype(jnp.bfloat16)
    row_count = gradient.shape[0]
    column_count = gradient.shape[1]
    for sweep_index in range(NS_STEPS):
        blocks = current.astype(jnp.float32).reshape(row_count, N_SEQ, column_count // N_SEQ)
        partial_grams = jnp.einsum('inb,jnb->nij', blocks, blocks).astype(jnp.bfloat16)
        gram_matrix = lax.optimization_barrier(jnp.sum(partial_grams.astype(jnp.float32), axis=0)).astype(jnp.bfloat16)
        square = jnp.dot(gram_matrix, gram_matrix, preferred_element_type=jnp.float32)
        mixing = (ns_second * gram_matrix.astype(jnp.float32) + ns_third * square).astype(jnp.bfloat16)
        current = (ns_first * current.astype(jnp.float32) + jnp.dot(mixing, current, preferred_element_type=jnp.float32)).astype(jnp.bfloat16)
    return current

def renormalize(weights, target_norms):
    return weights * (target_norms / (jnp.sqrt(lax.optimization_barrier(jnp.sum(weights * weights, axis=0))) + norm_eps))

def head_update(queries, key_rows, out_grad, fast, initial_norms):
    gate_fast, up_fast, down_fast = fast
    gate_low = gate_fast.astype(jnp.bfloat16)
    up_low = up_fast.astype(jnp.bfloat16)
    down_low = down_fast.astype(jnp.bfloat16)
    pre_gate = jnp.dot(key_rows, gate_low, preferred_element_type=jnp.float32)
    pre_up = jnp.dot(key_rows, up_low, preferred_element_type=jnp.float32)
    sigmoid_gate = jax.nn.sigmoid(pre_gate)
    gated = pre_gate * sigmoid_gate
    hidden = (gated * pre_up).astype(jnp.bfloat16)
    backward = jnp.dot(out_grad, down_low.T, preferred_element_type=jnp.float32)
    grad_gate = (backward * pre_up * sigmoid_gate * (1.0 + pre_gate * (1.0 - sigmoid_gate))).astype(jnp.bfloat16)
    grad_up = (backward * gated).astype(jnp.bfloat16)
    grad_first = jnp.dot(key_rows.T, grad_gate, preferred_element_type=jnp.float32)
    grad_third = jnp.dot(key_rows.T, grad_up, preferred_element_type=jnp.float32)
    grad_second = jnp.dot(out_grad.T, hidden, preferred_element_type=jnp.float32)
    gate_fast = renormalize(gate_fast - update_step * orthogonalize(grad_first).astype(jnp.float32), initial_norms[0])
    up_fast = renormalize(up_fast - update_step * orthogonalize(grad_third).astype(jnp.float32), initial_norms[1])
    down_fast = renormalize(down_fast - update_step * orthogonalize(grad_second).astype(jnp.float32).T, initial_norms[2])
    gate_out = jnp.dot(queries, gate_fast, precision=lax.Precision.HIGHEST)
    up_out = jnp.dot(queries, up_fast, precision=lax.Precision.HIGHEST)
    output = jnp.dot(jax.nn.silu(gate_out) * up_out, down_fast, precision=lax.Precision.HIGHEST)
    return (output, (gate_fast, up_fast, down_fast))

def run_section(residual, gain_row, qkv_weights, qk_gains, rate_row, out_gains, out_weights, fasts, norms):
    values = residual.astype(jnp.float32)
    normed = (rms_scale(values) * gain_row).astype(jnp.bfloat16)
    projected = jnp.dot(normed, qkv_weights.reshape(DM, HEADS * 3 * DH), preferred_element_type=jnp.float32)
    projected = projected.reshape(TOKENS, HEADS, 3, DH)
    mixed = jnp.zeros((TOKENS, DM), jnp.float32)
    new_fasts = []
    for head_index in range(HEADS):
        queries = rms_scale(projected[:, head_index, 0]) * qk_gains[head_index, 0]
        key_rows = (rms_scale(projected[:, head_index, 1]) * qk_gains[head_index, 1]).astype(jnp.bfloat16)
        out_grad = (-rate_row[:, None] * projected[:, head_index, 2]).astype(jnp.bfloat16)
        output, updated = head_update(queries, key_rows, out_grad, fasts[head_index], norms[head_index])
        normed_out = (rms_scale(output) * out_gains[head_index]).astype(jnp.bfloat16)
        mixed = mixed + jnp.dot(normed_out, out_weights[head_index], preferred_element_type=jnp.float32)
        new_fasts.append(updated)
    return ((values + mixed).astype(jnp.bfloat16), new_fasts)

def reference(stream, in_gain, w_qkv, qk_gain, w_one, w_three, w_two, token_rate, out_gain, w_out):
    results = []
    for section in range(SECTIONS):
        fasts = []
        norms = []
        for head_index in range(HEADS):
            weights = (w_one[section, head_index].astype(jnp.float32), w_three[section, head_index].astype(jnp.float32), w_two[section, head_index].astype(jnp.float32))
            fasts.append(weights)
            norms.append(tuple((jnp.sqrt(lax.optimization_barrier(jnp.sum(matrix * matrix, axis=0))) for matrix in weights)))
        section_out = []
        for span_index in range(SPANS):
            if section == 0:
                source = stream[span_index]
            else:
                source = results[section - 1][span_index]
            result, fasts = run_section(source, in_gain[section], w_qkv[section], qk_gain[section], token_rate[section, span_index], out_gain[section], w_out[section], fasts, norms)
            section_out.append(result)
        results.append(section_out)
    return jnp.stack([jnp.stack(section_out) for section_out in results])
```

```python
import jax
import jax.numpy as jnp
from jax import lax
from jax.sharding import Mesh
from jax.sharding import PartitionSpec as P

NS_STEPS = 2
SEQ = ("seq_0", "seq_1", "seq_2")

ns_first = 3.4445
ns_second = -4.775
ns_third = 2.0315
norm_eps = 1e-06
grad_eps = 1e-07


def turned(array, axis, by):
    devices = lax.axis_size(axis)
    return lax.ppermute(array, axis, [(i, (i + by) % devices) for i in range(devices)])


def others(array, axis):
    return [turned(array, axis, by) for by in range(1, lax.axis_size(axis))]


def gathered_columns(array, axis):
    devices = lax.axis_size(axis)
    here = lax.axis_index(axis)
    rows, width = array.shape
    whole = jnp.zeros((rows, devices, width), array.dtype)
    whole = lax.dynamic_update_index_in_dim(whole, array, here, 1)
    for by in range(1, devices):
        piece = turned(array, axis, by)
        whole = lax.dynamic_update_index_in_dim(whole, piece, (here - by) % devices, 1)
    return whole.reshape(rows, devices * width)


def summed_columns(array, axis):
    devices = lax.axis_size(axis)
    here = lax.axis_index(axis)
    rows, width = array.shape
    pieces = array.reshape(rows, devices, width // devices)
    own = lax.dynamic_index_in_dim(pieces, here, 1, keepdims=False)
    total = own
    for by in range(1, devices):
        piece = lax.dynamic_index_in_dim(pieces, (here + by) % devices, 1, keepdims=False)
        total = total + turned(piece.astype(jnp.bfloat16), axis, by).astype(jnp.float32)
    return total


def all_tokens(block):
    across = turned(block, "seq_0", 1)
    blocks = [block, *others(block, "seq_1"), across, *others(across, "seq_1")]
    mine = jnp.concatenate(blocks, axis=0)
    return jnp.concatenate([mine, turned(mine, "seq_2", 1)], axis=0)


def rms_scale(values):
    return values * lax.rsqrt(jnp.mean(values * values, axis=-1, keepdims=True) + norm_eps)


def contract_rows(left, right):
    return lax.dot_general(
        left, right, (((0,), (0,)), ((), ())), preferred_element_type=jnp.float32
    )


def contract_columns(left, right):
    return lax.dot_general(
        left, right, (((1,), (1,)), ((), ())), preferred_element_type=jnp.float32
    )


def orthogonal(gradient):
    current = (gradient / (jnp.sqrt(jnp.sum(gradient * gradient)) + grad_eps)).astype(jnp.bfloat16)
    for _ in range(NS_STEPS):
        gram = contract_columns(current, current).astype(jnp.bfloat16)
        square = jnp.dot(gram, gram, preferred_element_type=jnp.float32)
        mixing = (ns_second * gram.astype(jnp.float32) + ns_third * square).astype(jnp.bfloat16)
        current = (
            ns_first * current.astype(jnp.float32)
            + jnp.dot(mixing, current, preferred_element_type=jnp.float32)
        ).astype(jnp.bfloat16)
    return current.astype(jnp.float32)


def renormalize(weights, target_norms, axis):
    sums = jnp.sum(weights * weights, axis=axis, keepdims=True)
    return weights * (target_norms / (jnp.sqrt(sums) + norm_eps))


def project(whole, gain_row, qkv_matrix, head_gains, rate_row):
    normed = (rms_scale(whole.astype(jnp.float32)) * gain_row).astype(jnp.bfloat16)
    projected = jnp.dot(normed, qkv_matrix, preferred_element_type=jnp.float32)
    projected = projected.reshape(whole.shape[0], 3, -1)
    queries = rms_scale(projected[:, 0]) * head_gains[0]
    key_rows = (rms_scale(projected[:, 1]) * head_gains[1]).astype(jnp.bfloat16)
    out_grad = (-rate_row[:, None] * projected[:, 2]).astype(jnp.bfloat16)
    return queries, jnp.concatenate([key_rows, out_grad], axis=1)


def trained(tokens, queries, fasts, norms, out_gain_row):
    width = tokens.shape[1] // 2
    key_rows, out_grad = tokens[:, :width], tokens[:, width:]
    gate_low, up_low, down_low = (f.astype(jnp.bfloat16) for f in fasts)
    pre_gate = jnp.dot(key_rows, gate_low, preferred_element_type=jnp.float32)
    pre_up = jnp.dot(key_rows, up_low, preferred_element_type=jnp.float32)
    sigmoid_gate = jax.nn.sigmoid(pre_gate)
    gated = pre_gate * sigmoid_gate
    hidden = (gated * pre_up).astype(jnp.bfloat16)
    backward = jnp.dot(out_grad, down_low, preferred_element_type=jnp.float32)
    grad_gate = (backward * pre_up * sigmoid_gate * (1.0 + pre_gate * (1.0 - sigmoid_gate))).astype(
        jnp.bfloat16
    )
    grad_up = (backward * gated).astype(jnp.bfloat16)
    shares = (
        contract_rows(key_rows, grad_gate),
        contract_rows(key_rows, grad_up),
        contract_rows(out_grad, hidden),
    )
    fresh = tuple(
        renormalize(fast - orthogonal(share), norm, axis)
        for fast, share, norm, axis in zip(fasts, shares, norms, (0, 0, 1))
    )
    gate_low, up_low, down_low = (f.astype(jnp.bfloat16) for f in fresh)
    queries = queries.astype(jnp.bfloat16)
    gate_out = jnp.dot(queries, gate_low, preferred_element_type=jnp.float32)
    up_out = jnp.dot(queries, up_low, preferred_element_type=jnp.float32)
    output = contract_columns((jax.nn.silu(gate_out) * up_out).astype(jnp.bfloat16), down_low)
    return (rms_scale(output) * out_gain_row).astype(jnp.bfloat16), fresh


def shards(stream, in_gain, w_qkv, qk_gain, w_one, w_three, w_two, token_rate, out_gain, w_out):
    segment_index = lax.axis_index("segment")
    span_count = stream.shape[0]
    qkv_matrix = w_qkv[0].reshape(w_qkv.shape[1], -1)
    initial = (
        w_one[0, 0].astype(jnp.float32),
        w_three[0, 0].astype(jnp.float32),
        w_two[0, 0].T.astype(jnp.float32),
    )
    norms = tuple(
        jnp.sqrt(jnp.sum(matrix * matrix, axis=axis, keepdims=True))
        for matrix, axis in zip(initial, (0, 0, 1))
    )

    def section(sources):
        prepared = []
        for span, source in enumerate(sources):
            queries, own = project(
                gathered_columns(source, "head"),
                in_gain[0],
                qkv_matrix,
                qk_gain[0, 0],
                token_rate[0, span],
            )
            prepared.append((queries, all_tokens(own)))
        fasts, results = initial, []
        for (queries, tokens), source in zip(prepared, sources):
            normed_out, fasts = trained(tokens, queries, fasts, norms, out_gain[0, 0])
            head_terms = jnp.dot(normed_out, w_out[0, 0], preferred_element_type=jnp.float32)
            delta = summed_columns(head_terms, "head")
            results.append((source.astype(jnp.float32) + delta).astype(jnp.bfloat16))
        return results

    results = section([stream[span] for span in range(span_count)])
    for _ in range(1, lax.axis_size("segment")):
        step = lax.axis_size("segment") - 1
        received = [lax.ppermute(r, "segment", [(i, i + 1) for i in range(step)]) for r in results]
        later = section(received)
        results = [
            jnp.where(segment_index == 0, r, fresh) for r, fresh in zip(results, later)
        ]
    return jnp.stack(results)[None]


def solution(mesh):
    torus = Mesh(
        mesh.devices.reshape(mesh.shape["segment"], 2, 4, 2, mesh.shape["head"]),
        ("segment", "seq_0", "seq_1", "seq_2", "head"),
    )
    return jax.shard_map(
        shards,
        mesh=torus,
        in_specs=(
            P(None, SEQ, "head"),
            P("segment", None),
            P("segment", None, "head", None, None),
            P("segment", "head", None, None),
            P("segment", "head", None, None),
            P("segment", "head", None, None),
            P("segment", "head", None, None),
            P("segment", None, SEQ),
            P("segment", "head", None),
            P("segment", "head", None, None),
        ),
        out_specs=P("segment", None, SEQ, "head"),
        check_vma=False,
    )
```

```python
import jax
import jax.numpy as jnp
from jax import lax
from jax.experimental import pallas as pl
from jax.experimental.pallas import tpu as pltpu
from jax.sharding import Mesh
from jax.sharding import PartitionSpec as P

NS_STEPS = 2
SEQ = ("seq_0", "seq_1", "seq_2")

ns_first = 3.4445
ns_second = -4.775
ns_third = 2.0315
norm_eps = 1e-06
grad_eps = 1e-07


def turned(array, axis, by):
    devices = lax.axis_size(axis)
    return lax.ppermute(array, axis, [(i, (i + by) % devices) for i in range(devices)])


def others(array, axis):
    return [turned(array, axis, by) for by in range(1, lax.axis_size(axis))]


def gathered_columns(array, axis):
    devices = lax.axis_size(axis)
    here = lax.axis_index(axis)
    rows, width = array.shape
    whole = jnp.zeros((rows, devices, width), array.dtype)
    whole = lax.dynamic_update_index_in_dim(whole, array, here, 1)
    for by in range(1, devices):
        piece = turned(array, axis, by)
        whole = lax.dynamic_update_index_in_dim(whole, piece, (here - by) % devices, 1)
    return whole.reshape(rows, devices * width)


def summed_columns(array, axis):
    devices = lax.axis_size(axis)
    here = lax.axis_index(axis)
    rows, width = array.shape
    pieces = array.reshape(rows, devices, width // devices)
    own = lax.dynamic_index_in_dim(pieces, here, 1, keepdims=False)
    total = own
    for by in range(1, devices):
        piece = lax.dynamic_index_in_dim(pieces, (here + by) % devices, 1, keepdims=False)
        total = total + turned(piece.astype(jnp.bfloat16), axis, by).astype(jnp.float32)
    return total


def all_tokens(block):
    across = turned(block, "seq_0", 1)
    blocks = [block, *others(block, "seq_1"), across, *others(across, "seq_1")]
    mine = jnp.concatenate(blocks, axis=0)
    return jnp.concatenate([mine, turned(mine, "seq_2", 1)], axis=0)


def rms_scale(values):
    return values * lax.rsqrt(jnp.mean(values * values, axis=-1, keepdims=True) + norm_eps)


def contract_columns(left, right):
    return lax.dot_general(
        left, right, (((1,), (1,)), ((), ())), preferred_element_type=jnp.float32
    )


def product(left, right):
    return jnp.dot(left, right, preferred_element_type=jnp.float32)


def project(whole, gain_row, qkv_matrix, head_gains, rate_row):
    normed = (rms_scale(whole.astype(jnp.float32)) * gain_row).astype(jnp.bfloat16)
    projected = jnp.dot(normed, qkv_matrix, preferred_element_type=jnp.float32)
    projected = projected.reshape(whole.shape[0], 3, -1)
    queries = rms_scale(projected[:, 0]) * head_gains[0]
    key_rows = (rms_scale(projected[:, 1]) * head_gains[1]).astype(jnp.bfloat16)
    out_grad = (-rate_row[:, None] * projected[:, 2]).astype(jnp.bfloat16)
    return queries, jnp.concatenate([key_rows, out_grad], axis=1)


def update_kernel(
    tokens,
    queries,
    gate,
    up,
    down,
    gate_norm,
    up_norm,
    down_norm,
    out_gain,
    normed_out,
    gate_new,
    up_new,
    down_new,
    lows,
    turned_keys,
    turned_grads,
    grads,
    shares,
    iterate,
):
    count, width = tokens.shape[0], queries.shape[1]
    inner = gate.shape[1]
    rows, columns = 512, 256
    lows[0] = gate[...].astype(jnp.bfloat16)
    lows[1] = up[...].astype(jnp.bfloat16)
    lows[2] = down[...].astype(jnp.bfloat16)

    @pl.loop(0, count // rows)
    def _(step):
        lines = pl.ds(pl.multiple_of(step * rows, rows), rows)
        key_rows = tokens[lines, :width]
        out_grad = tokens[lines, width:]
        turned_keys[:, lines] = key_rows.T
        turned_grads[:, lines] = out_grad.T
        for start in range(0, inner, columns):
            part = slice(start, start + columns)
            pre_gate = product(key_rows, lows[0, :, part])
            pre_up = product(key_rows, lows[1, :, part])
            backward = product(out_grad, lows[2, :, part])
            sigmoid_gate = 0.5 + 0.5 * jnp.tanh(0.5 * pre_gate)
            gated = pre_gate * sigmoid_gate
            slope = sigmoid_gate + gated * (1.0 - sigmoid_gate)
            grads[0, lines, part] = (backward * pre_up * slope).astype(jnp.bfloat16)
            grads[1, lines, part] = (backward * gated).astype(jnp.bfloat16)
            grads[2, lines, part] = (gated * pre_up).astype(jnp.bfloat16)

    for index, left in enumerate((turned_keys, turned_keys, turned_grads)):
        squares = jnp.zeros((1, columns), jnp.float32)
        for start in range(0, inner, columns):
            part = slice(start, start + columns)
            share = product(left[...], grads[index, :, part])
            squares = squares + jnp.sum(share * share, axis=0, keepdims=True)
            shares[index, :, part] = share
        total = jnp.sum(squares, axis=1, keepdims=True)
        scale = 1.0 / (jnp.sqrt(total) + grad_eps)
        iterate[index] = (shares[index] * scale).astype(jnp.bfloat16)

    for _ in range(NS_STEPS):
        for index in range(3):
            block = iterate[index]
            gram = contract_columns(block, block).astype(jnp.bfloat16)
            square = product(gram, gram)
            mixing = (ns_second * gram.astype(jnp.float32) + ns_third * square).astype(jnp.bfloat16)
            moved = product(mixing, block)
            iterate[index] = (ns_first * block.astype(jnp.float32) + moved).astype(jnp.bfloat16)

    fresh = []
    for index, (fast, norm, result, axis) in enumerate(
        (
            (gate, gate_norm, gate_new, 0),
            (up, up_norm, up_new, 0),
            (down, down_norm, down_new, 1),
        )
    ):
        moved = fast[...] - iterate[index].astype(jnp.float32)
        sums = jnp.sum(moved * moved, axis=axis, keepdims=True)
        moved = moved * (norm[...] / (jnp.sqrt(sums) + norm_eps))
        result[...] = moved
        fresh.append(moved.astype(jnp.bfloat16))
    gate_low, up_low, down_low = fresh
    low_queries = queries[...].astype(jnp.bfloat16)
    gate_out = product(low_queries, gate_low)
    up_out = product(low_queries, up_low)
    hidden = gate_out * (0.5 + 0.5 * jnp.tanh(0.5 * gate_out)) * up_out
    output = contract_columns(hidden.astype(jnp.bfloat16), down_low)
    normed_out[...] = (rms_scale(output) * out_gain[...]).astype(jnp.bfloat16)


def trained(tokens, queries, fasts, norms, out_gain_row):
    count = tokens.shape[0]
    width, inner = fasts[0].shape
    whole = pl.BlockSpec(memory_space=pltpu.VMEM)
    results = pl.pallas_call(
        update_kernel,
        out_shape=[
            jax.ShapeDtypeStruct(queries.shape, jnp.bfloat16),
            *(jax.ShapeDtypeStruct(fast.shape, jnp.float32) for fast in fasts),
        ],
        in_specs=[whole] * 9,
        out_specs=[whole] * 4,
        scratch_shapes=[
            pltpu.VMEM((3, width, inner), jnp.bfloat16),
            pltpu.VMEM((width, count), jnp.bfloat16),
            pltpu.VMEM((width, count), jnp.bfloat16),
            pltpu.VMEM((3, count, inner), jnp.bfloat16),
            pltpu.VMEM((3, width, inner), jnp.float32),
            pltpu.VMEM((3, width, inner), jnp.bfloat16),
        ],
        compiler_params=pltpu.CompilerParams(vmem_limit_bytes=50 * 2**20),
        cost_estimate=pl.CostEstimate(
            flops=12 * count * width * inner + 12 * width * width * (2 * inner + width),
            bytes_accessed=32 * width * inner,
            transcendentals=count * inner,
        ),
        name="update",
    )(tokens, queries, *fasts, *norms, out_gain_row)
    return results[0], tuple(results[1:])


def shards(stream, in_gain, w_qkv, qk_gain, w_one, w_three, w_two, token_rate, out_gain, w_out):
    segment_index = lax.axis_index("segment")
    span_count = stream.shape[0]
    qkv_matrix = w_qkv[0].reshape(w_qkv.shape[1], -1)
    initial = (
        w_one[0, 0].astype(jnp.float32),
        w_three[0, 0].astype(jnp.float32),
        w_two[0, 0].T.astype(jnp.float32),
    )
    norms = tuple(
        jnp.sqrt(jnp.sum(matrix * matrix, axis=axis, keepdims=True))
        for matrix, axis in zip(initial, (0, 0, 1))
    )

    def section(sources):
        prepared = []
        for span, source in enumerate(sources):
            queries, own = project(
                gathered_columns(source, "head"),
                in_gain[0],
                qkv_matrix,
                qk_gain[0, 0],
                token_rate[0, span],
            )
            prepared.append((queries, all_tokens(own)))
        fasts, results = initial, []
        for (queries, tokens), source in zip(prepared, sources):
            normed_out, fasts = trained(tokens, queries, fasts, norms, out_gain[0])
            head_terms = jnp.dot(normed_out, w_out[0, 0], preferred_element_type=jnp.float32)
            delta = summed_columns(head_terms, "head")
            results.append((source.astype(jnp.float32) + delta).astype(jnp.bfloat16))
        return results

    results = section([stream[span] for span in range(span_count)])
    for _ in range(1, lax.axis_size("segment")):
        step = lax.axis_size("segment") - 1
        received = [lax.ppermute(r, "segment", [(i, i + 1) for i in range(step)]) for r in results]
        later = section(received)
        results = [
            jnp.where(segment_index == 0, r, fresh) for r, fresh in zip(results, later)
        ]
    return jnp.stack(results)[None]


def solution(mesh):
    torus = Mesh(
        mesh.devices.reshape(mesh.shape["segment"], 2, 4, 2, mesh.shape["head"]),
        ("segment", "seq_0", "seq_1", "seq_2", "head"),
    )
    return jax.shard_map(
        shards,
        mesh=torus,
        in_specs=(
            P(None, SEQ, "head"),
            P("segment", None),
            P("segment", None, "head", None, None),
            P("segment", "head", None, None),
            P("segment", "head", None, None),
            P("segment", "head", None, None),
            P("segment", "head", None, None),
            P("segment", None, SEQ),
            P("segment", "head", None),
            P("segment", "head", None, None),
        ),
        out_specs=P("segment", None, SEQ, "head"),
        check_vma=False,
    )
```

```python
import jax
import jax.numpy as jnp
from jax import lax
from jax.experimental import pallas as pl
from jax.experimental.pallas import tpu as pltpu
from jax.sharding import Mesh
from jax.sharding import PartitionSpec as P

NS_STEPS = 2
SEQ = ("seq_0", "seq_1", "seq_2")

ns_first = 3.4445
ns_second = -4.775
ns_third = 2.0315
norm_eps = 1e-06
grad_eps = 1e-07


def turned(array, axis, by, segment):
    devices = lax.axis_size(axis)
    first = segment * devices
    pairs = [(first + i, first + (i + by) % devices) for i in range(devices)]
    return lax.ppermute(array, ("segment", axis), pairs)


def others(array, axis, segment):
    return [turned(array, axis, by, segment) for by in range(1, lax.axis_size(axis))]


def summed_columns(array, axis, segment):
    devices = lax.axis_size(axis)
    here = lax.axis_index(axis)
    width = array.shape[1] // devices

    def piece(index):
        return lax.dynamic_slice_in_dim(array, index * width, width, 1)

    total = piece(here)
    for by in range(1, devices):
        sent = piece((here + by) % devices).astype(jnp.bfloat16)
        total = total + turned(sent, axis, by, segment).astype(jnp.float32)
    return total


def all_tokens(block, segment):
    near = [block, *others(block, "seq_1", segment)]
    across = turned(block, "seq_0", 1, segment)
    far = [across, *others(across, "seq_1", segment)]
    blocks = near + far
    return near, blocks + [turned(b, "seq_2", 1, segment) for b in blocks]


def rms_scale(values):
    return values * lax.rsqrt(jnp.mean(values * values, axis=-1, keepdims=True) + norm_eps)


def contract_columns(left, right):
    return lax.dot_general(
        left, right, (((1,), (1,)), ((), ())), preferred_element_type=jnp.float32
    )


def product(left, right):
    return jnp.dot(left, right, preferred_element_type=jnp.float32)


def project_kernel(places, *refs):
    blocks = refs[:-8]
    gain, weights, head_gains, rates, queries, pairs, total, scale = refs[-8:]
    step = pl.program_id(0)
    steps = pl.num_programs(0)
    active = places[len(blocks)] == 1
    width = queries.shape[1]
    features = weights.shape[0]
    parts = blocks[0].shape[1] // features

    @pl.when((step == 0) & active)
    def _():
        squares = jnp.zeros(scale.shape, jnp.float32)
        for block in blocks:
            values = block[...].astype(jnp.float32)
            squares = squares + jnp.sum(values * values, axis=1, keepdims=True)
        count = len(blocks) * blocks[0].shape[1]
        scale[...] = lax.rsqrt(squares / count + norm_eps)
        total[...] = jnp.zeros_like(total)

    for index in range(len(blocks) * parts):

        @pl.when((step == index) & active)
        def _():
            start = index % parts * features
            values = blocks[index // parts][:, start : start + features].astype(jnp.float32)
            normed = (values * scale[...] * gain[...]).astype(jnp.bfloat16)
            total[...] += product(normed, weights[...])

    @pl.when((step == steps - 1) & active)
    def _():
        queries[...] = (rms_scale(total[:, :width]) * head_gains[0:1, :]).astype(jnp.bfloat16)
        key_rows = rms_scale(total[:, width : 2 * width]) * head_gains[1:2, :]
        pairs[:, :width] = key_rows.astype(jnp.bfloat16)
        pairs[:, width:] = (-rates[...] * total[:, 2 * width :]).astype(jnp.bfloat16)

    @pl.when((step == steps - 1) & jnp.logical_not(active))
    def _():
        queries[...] = jnp.zeros_like(queries)
        pairs[...] = jnp.zeros_like(pairs)


def project(source, gain_row, qkv_matrix, head_gains, rate_row, segment):
    blocks = [source, *others(source, "head", segment)]
    rows, columns = source.shape
    width = head_gains.shape[1]
    features = 512
    parts = columns // features
    heads = len(blocks)
    here = lax.axis_index("head")
    active = (lax.axis_index("segment") == segment).astype(jnp.int32)
    places = jnp.stack([(here - by) % heads for by in range(heads)] + [active])

    def place(step, places):
        return (places[step // parts] * parts + step % parts) * places[heads]

    def whole(*dims):
        return pl.BlockSpec(dims, lambda step, places: (0,) * len(dims))

    return pl.pallas_call(
        project_kernel,
        grid_spec=pltpu.PrefetchScalarGridSpec(
            num_scalar_prefetch=1,
            grid=(heads * parts,),
            in_specs=[
                *[whole(rows, columns)] * heads,
                pl.BlockSpec((1, features), lambda step, places: (0, place(step, places))),
                pl.BlockSpec((features, 3 * width), lambda step, places: (place(step, places), 0)),
                whole(2, width),
                whole(rows, 1),
            ],
            out_specs=[whole(rows, width), whole(rows, 2 * width)],
            scratch_shapes=[
                pltpu.VMEM((rows, 3 * width), jnp.float32),
                pltpu.VMEM((rows, 1), jnp.float32),
            ],
        ),
        out_shape=[
            jax.ShapeDtypeStruct((rows, width), jnp.bfloat16),
            jax.ShapeDtypeStruct((rows, 2 * width), jnp.bfloat16),
        ],
        compiler_params=pltpu.CompilerParams(
            dimension_semantics=("arbitrary",), vmem_limit_bytes=20 * 2**20
        ),
        cost_estimate=pl.CostEstimate(
            flops=6 * rows * columns * heads * width,
            bytes_accessed=6 * columns * heads * width,
            transcendentals=0,
        ),
        name="project",
    )(places, *blocks, gain_row, qkv_matrix, head_gains, rate_row)


def update_kernel(active, *refs):
    normed_out = refs[-11]

    @pl.when(active[0] == 1)
    def _():
        update(refs[:-19], *refs[-19:])

    @pl.when(active[0] != 1)
    def _():
        normed_out[...] = jnp.zeros_like(normed_out)


def update(
    blocks,
    queries,
    gate,
    up,
    down,
    gate_norm,
    up_norm,
    down_norm,
    out_gain,
    normed_out,
    gate_new,
    up_new,
    down_new,
    tokens,
    lows,
    turned_keys,
    turned_grads,
    grads,
    shares,
    iterate,
):
    count, width = tokens.shape[0], queries.shape[1]
    inner = gate.shape[1]
    rows, columns = 512, 256
    for index, block in enumerate(blocks):
        tokens[pl.ds(index * block.shape[0], block.shape[0]), :] = block[...]
    lows[0] = gate[...].astype(jnp.bfloat16)
    lows[1] = up[...].astype(jnp.bfloat16)
    lows[2] = down[...].astype(jnp.bfloat16)

    @pl.loop(0, count // rows)
    def _(step):
        lines = pl.ds(pl.multiple_of(step * rows, rows), rows)
        key_rows = tokens[lines, :width]
        out_grad = tokens[lines, width:]
        turned_keys[:, lines] = key_rows.T
        turned_grads[:, lines] = out_grad.T
        for start in range(0, inner, columns):
            part = slice(start, start + columns)
            pre_gate = product(key_rows, lows[0, :, part])
            pre_up = product(key_rows, lows[1, :, part])
            backward = product(out_grad, lows[2, :, part])
            sigmoid_gate = 0.5 + 0.5 * jnp.tanh(0.5 * pre_gate)
            gated = pre_gate * sigmoid_gate
            slope = sigmoid_gate + gated * (1.0 - sigmoid_gate)
            grads[0, lines, part] = (backward * pre_up * slope).astype(jnp.bfloat16)
            grads[1, lines, part] = (backward * gated).astype(jnp.bfloat16)
            grads[2, lines, part] = (gated * pre_up).astype(jnp.bfloat16)

    for index, left in enumerate((turned_keys, turned_keys, turned_grads)):
        squares = jnp.zeros((1, columns), jnp.float32)
        for start in range(0, inner, columns):
            part = slice(start, start + columns)
            share = product(left[...], grads[index, :, part])
            squares = squares + jnp.sum(share * share, axis=0, keepdims=True)
            shares[index, :, part] = share
        total = jnp.sum(squares, axis=1, keepdims=True)
        scale = 1.0 / (jnp.sqrt(total) + grad_eps)
        iterate[index] = (shares[index] * scale).astype(jnp.bfloat16)

    for _ in range(NS_STEPS):
        for index in range(3):
            block = iterate[index]
            gram = contract_columns(block, block).astype(jnp.bfloat16)
            square = product(gram, gram)
            mixing = (ns_second * gram.astype(jnp.float32) + ns_third * square).astype(jnp.bfloat16)
            moved = product(mixing, block)
            iterate[index] = (ns_first * block.astype(jnp.float32) + moved).astype(jnp.bfloat16)

    fresh = []
    for index, (fast, norm, result, axis) in enumerate(
        (
            (gate, gate_norm, gate_new, 0),
            (up, up_norm, up_new, 0),
            (down, down_norm, down_new, 1),
        )
    ):
        moved = fast[...] - iterate[index].astype(jnp.float32)
        sums = jnp.sum(moved * moved, axis=axis, keepdims=True)
        moved = moved * (norm[...] / (jnp.sqrt(sums) + norm_eps))
        result[...] = moved
        fresh.append(moved.astype(jnp.bfloat16))
    gate_low, up_low, down_low = fresh
    low_queries = queries[...]
    gate_out = product(low_queries, gate_low)
    up_out = product(low_queries, up_low)
    hidden = gate_out * (0.5 + 0.5 * jnp.tanh(0.5 * gate_out)) * up_out
    output = contract_columns(hidden.astype(jnp.bfloat16), down_low)
    normed_out[...] = (rms_scale(output) * out_gain[...]).astype(jnp.bfloat16)


def trained(blocks, queries, fasts, norms, out_gain_row, active):
    rows = blocks[0].shape[0]
    count = rows * len(blocks)
    width, inner = fasts[0].shape
    whole = pl.BlockSpec(memory_space=pltpu.VMEM)
    results = pl.pallas_call(
        update_kernel,
        out_shape=[
            jax.ShapeDtypeStruct(queries.shape, jnp.bfloat16),
            *(jax.ShapeDtypeStruct(fast.shape, jnp.float32) for fast in fasts),
        ],
        in_specs=[pl.BlockSpec(memory_space=pltpu.SMEM)] + [whole] * (len(blocks) + 8),
        out_specs=[whole] * 4,
        scratch_shapes=[
            pltpu.VMEM((count, 2 * width), jnp.bfloat16),
            pltpu.VMEM((3, width, inner), jnp.bfloat16),
            pltpu.VMEM((width, count), jnp.bfloat16),
            pltpu.VMEM((width, count), jnp.bfloat16),
            pltpu.VMEM((3, count, inner), jnp.bfloat16),
            pltpu.VMEM((3, width, inner), jnp.float32),
            pltpu.VMEM((3, width, inner), jnp.bfloat16),
        ],
        compiler_params=pltpu.CompilerParams(vmem_limit_bytes=52 * 2**20),
        cost_estimate=pl.CostEstimate(
            flops=12 * count * width * inner + 12 * width * width * (2 * inner + width),
            bytes_accessed=32 * width * inner,
            transcendentals=count * inner,
        ),
        name="update",
    )(active, *blocks, queries, *fasts, *norms, out_gain_row)
    return results[0], tuple(results[1:])


def shards(stream, in_gain, w_qkv, qk_gain, w_one, w_three, w_two, token_rate, out_gain, w_out):
    segment_index = lax.axis_index("segment")
    span_count = stream.shape[0]
    qkv_matrix = w_qkv[0].reshape(w_qkv.shape[1], -1)
    initial = (
        w_one[0, 0].astype(jnp.float32),
        w_three[0, 0].astype(jnp.float32),
        w_two[0, 0].T.astype(jnp.float32),
    )
    norms = tuple(
        jnp.sqrt(jnp.sum(matrix * matrix, axis=axis, keepdims=True))
        for matrix, axis in zip(initial, (0, 0, 1))
    )

    last = lax.axis_size("segment") - 1
    sources = [stream[span] for span in range(span_count)]
    results = None
    for segment in range(last + 1):
        active = (segment_index == segment).astype(jnp.int32)[None]

        def prepared(source, span):
            queries, own = project(
                source,
                in_gain,
                qkv_matrix,
                qk_gain[0, 0],
                token_rate[0, span][:, None],
                segment,
            )
            return (queries, *all_tokens(own, segment))

        fasts, outcome, received = initial, [], []
        ready = prepared(sources[0], 0)
        for span in range(span_count):
            queries, _, blocks = ready
            if span + 1 < span_count:
                following = sources[span + 1]
                near, following = lax.optimization_barrier((ready[1], following))
                ready = prepared(following, span + 1)
                held, later = lax.optimization_barrier((blocks[-1], ready[0]))
                blocks = blocks[:-1] + [held]
                ready = (later, *ready[1:])
            if received:
                held, received[-1] = lax.optimization_barrier((blocks[-1], received[-1]))
                blocks = blocks[:-1] + [held]
            normed_out, fasts = trained(blocks, queries, fasts, norms, out_gain[0], active)
            head_terms = product(normed_out, w_out[0, 0])
            delta = summed_columns(head_terms, "head", segment)
            outcome.append((sources[span].astype(jnp.float32) + delta).astype(jnp.bfloat16))
            if segment < last:
                received.append(lax.ppermute(outcome[-1], "segment", [(segment, segment + 1)]))
        chosen = segment_index == segment
        results = (
            outcome
            if results is None
            else [jnp.where(chosen, fresh, former) for fresh, former in zip(outcome, results)]
        )
        sources = received
    return jnp.stack(results)[None]


def solution(mesh):
    torus = Mesh(
        mesh.devices.reshape(mesh.shape["segment"], 2, 4, 2, mesh.shape["head"]),
        ("segment", "seq_0", "seq_1", "seq_2", "head"),
    )
    return jax.shard_map(
        shards,
        mesh=torus,
        in_specs=(
            P(None, SEQ, "head"),
            P("segment", None),
            P("segment", None, "head", None, None),
            P("segment", "head", None, None),
            P("segment", "head", None, None),
            P("segment", "head", None, None),
            P("segment", "head", None, None),
            P("segment", None, SEQ),
            P("segment", "head", None),
            P("segment", "head", None, None),
        ),
        out_specs=P("segment", None, SEQ, "head"),
        check_vma=False,
    )
```

```python
import jax
import jax.numpy as jnp
from jax import lax
from jax.experimental import pallas as pl
from jax.experimental.pallas import tpu as pltpu
from jax.sharding import Mesh
from jax.sharding import PartitionSpec as P

NS_STEPS = 2
SEQ = ("seq_0", "seq_1", "seq_2")

ns_first = 3.4445
ns_second = -4.775
ns_third = 2.0315
norm_eps = 1e-06
grad_eps = 1e-07


def turned(array, axis, by):
    devices = lax.axis_size(axis)
    return lax.ppermute(array, axis, [(i, (i + by) % devices) for i in range(devices)])


def others(array, axis):
    return [turned(array, axis, by) for by in range(1, lax.axis_size(axis))]


def summed_columns(array, axis):
    devices = lax.axis_size(axis)
    here = lax.axis_index(axis)
    width = array.shape[1] // devices

    def piece(index):
        return lax.dynamic_slice_in_dim(array, index * width, width, 1)

    total = piece(here)
    for by in range(1, devices):
        sent = piece((here + by) % devices).astype(jnp.bfloat16)
        total = total + turned(sent, axis, by).astype(jnp.float32)
    return total


def own_core_tokens(block):
    near = [block, *others(block, "seq_1")]
    across = turned(block, "seq_0", 1)
    return near + [across], others(across, "seq_1")


def rms_scale(values):
    return values * lax.rsqrt(jnp.mean(values * values, axis=-1, keepdims=True) + norm_eps)


def contract_columns(left, right):
    return lax.dot_general(
        left, right, (((1,), (1,)), ((), ())), preferred_element_type=jnp.float32
    )


def product(left, right):
    return jnp.dot(left, right, preferred_element_type=jnp.float32)


def project_kernel(places, *refs):
    blocks = refs[:-8]
    gain, weights, head_gains, rates, queries, pairs, total, scale = refs[-8:]
    step = pl.program_id(0)
    steps = pl.num_programs(0)
    active = places[len(blocks)] == 1
    width = queries.shape[1]
    features = weights.shape[1]
    parts = blocks[0].shape[1] // features

    @pl.when((step == 0) & active)
    def _():
        squares = jnp.zeros(scale.shape, jnp.float32)
        for block in blocks:
            values = block[...].astype(jnp.float32)
            squares = squares + jnp.sum(values * values, axis=1, keepdims=True)
        count = len(blocks) * blocks[0].shape[1]
        scale[...] = lax.rsqrt(squares / count + norm_eps)
        total[...] = jnp.zeros_like(total)

    for index in range(len(blocks) * parts):

        @pl.when((step == index) & active)
        def _():
            start = index % parts * features
            values = blocks[index // parts][:, start : start + features].astype(jnp.float32)
            normed = (values * scale[...] * gain[...]).astype(jnp.bfloat16)
            for third in range(3):
                part = slice(third * width, (third + 1) * width)
                total[:, part] += product(normed, weights[third])

    @pl.when((step == steps - 1) & active)
    def _():
        queries[...] = (rms_scale(total[:, :width]) * head_gains[0:1, :]).astype(jnp.bfloat16)
        key_rows = rms_scale(total[:, width : 2 * width]) * head_gains[1:2, :]
        pairs[:, :width] = key_rows.astype(jnp.bfloat16)
        pairs[:, width:] = (-rates[...] * total[:, 2 * width :]).astype(jnp.bfloat16)

    @pl.when((step == steps - 1) & jnp.logical_not(active))
    def _():
        queries[...] = jnp.zeros_like(queries)
        pairs[...] = jnp.zeros_like(pairs)


def project(source, gain_row, qkv_matrix, head_gains, rate_row, segment):
    blocks = [source, *others(source, "head")]
    rows, columns = source.shape
    width = head_gains.shape[1]
    features = 512
    parts = columns // features
    heads = len(blocks)
    here = lax.axis_index("head")
    active = (lax.axis_index("segment") == segment).astype(jnp.int32)
    places = jnp.stack([(here - by) % heads for by in range(heads)] + [active])

    def place(step, places):
        return (places[step // parts] * parts + step % parts) * places[heads]

    def whole(*dims):
        return pl.BlockSpec(dims, lambda step, places: (0,) * len(dims))

    return pl.pallas_call(
        project_kernel,
        grid_spec=pltpu.PrefetchScalarGridSpec(
            num_scalar_prefetch=1,
            grid=(heads * parts,),
            in_specs=[
                *[whole(rows, columns)] * heads,
                pl.BlockSpec((1, features), lambda step, places: (0, place(step, places))),
                pl.BlockSpec(
                    (3, features, width), lambda step, places: (0, place(step, places), 0)
                ),
                whole(2, width),
                whole(rows, 1),
            ],
            out_specs=[whole(rows, width), whole(rows, 2 * width)],
            scratch_shapes=[
                pltpu.VMEM((rows, 3 * width), jnp.float32),
                pltpu.VMEM((rows, 1), jnp.float32),
            ],
        ),
        out_shape=[
            jax.ShapeDtypeStruct((rows, width), jnp.bfloat16),
            jax.ShapeDtypeStruct((rows, 2 * width), jnp.bfloat16),
        ],
        compiler_params=pltpu.CompilerParams(
            dimension_semantics=("arbitrary",), vmem_limit_bytes=20 * 2**20
        ),
        cost_estimate=pl.CostEstimate(
            flops=6 * rows * columns * heads * width,
            bytes_accessed=6 * columns * heads * width,
            transcendentals=0,
        ),
        name="project",
    )(places, *blocks, gain_row, qkv_matrix, head_gains, rate_row)


def gradient_kernel(active, *refs):
    blocks = refs[:-9]
    gate, up, down, shares, tokens, turned_keys, turned_grads, grads, _ = refs[-9:]

    @pl.when(active[0] == 1)
    def _():
        count, width = tokens.shape[0], gate.shape[0]
        inner = gate.shape[1]
        rows, columns = 512, 256
        for index, block in enumerate(blocks):
            tokens[pl.ds(index * block.shape[0], block.shape[0]), :] = block[...]

        @pl.loop(0, count // rows)
        def _(step):
            lines = pl.ds(pl.multiple_of(step * rows, rows), rows)
            key_rows = tokens[lines, :width]
            out_grad = tokens[lines, width:]
            turned_keys[:, lines] = key_rows.T
            turned_grads[:, lines] = out_grad.T
            for start in range(0, inner, columns):
                part = slice(start, start + columns)
                pre_gate = product(key_rows, gate[:, part])
                pre_up = product(key_rows, up[:, part])
                backward = product(out_grad, down[:, part])
                sigmoid_gate = 0.5 + 0.5 * jnp.tanh(0.5 * pre_gate)
                gated = pre_gate * sigmoid_gate
                slope = sigmoid_gate + gated * (1.0 - sigmoid_gate)
                grads[0, lines, part] = (backward * pre_up * slope).astype(jnp.bfloat16)
                grads[1, lines, part] = (backward * gated).astype(jnp.bfloat16)
                grads[2, lines, part] = (gated * pre_up).astype(jnp.bfloat16)

        for index, left in enumerate((turned_keys, turned_keys, turned_grads)):
            for start in range(0, inner, columns):
                part = slice(start, start + columns)
                share = product(left[...], grads[index, :, part])
                shares[index, :, part] = share.astype(jnp.bfloat16)


def gradient_shares(blocks, fasts, active):
    count = blocks[0].shape[0] * len(blocks)
    width, inner = fasts[0].shape
    whole = pl.BlockSpec(memory_space=pltpu.VMEM)
    return pl.pallas_call(
        gradient_kernel,
        out_shape=jax.ShapeDtypeStruct((3, width, inner), jnp.bfloat16),
        in_specs=[pl.BlockSpec(memory_space=pltpu.SMEM)] + [whole] * (len(blocks) + 3),
        out_specs=whole,
        scratch_shapes=[
            pltpu.VMEM((count, 2 * width), jnp.bfloat16),
            pltpu.VMEM((width, count), jnp.bfloat16),
            pltpu.VMEM((width, count), jnp.bfloat16),
            pltpu.VMEM((3, count, inner), jnp.bfloat16),
            pltpu.VMEM((8, 128), jnp.float32),
        ],
        compiler_params=pltpu.CompilerParams(vmem_limit_bytes=30 * 2**20),
        cost_estimate=pl.CostEstimate(
            flops=12 * count * width * inner,
            bytes_accessed=12 * width * inner,
            transcendentals=count * inner,
        ),
        name="gradients",
    )(active, *blocks, *fasts)


def update_kernel(active, *refs):
    normed_out = refs[10]

    @pl.when(active[0] == 1)
    def _():
        update(*refs)

    @pl.when(active[0] != 1)
    def _():
        normed_out[...] = jnp.zeros_like(normed_out)


def update(
    shares,
    other_shares,
    queries,
    gate,
    up,
    down,
    gate_norm,
    up_norm,
    down_norm,
    out_gain,
    normed_out,
    gate_new,
    up_new,
    down_new,
    iterate,
):
    for index in range(3):
        share = shares[index].astype(jnp.float32) + other_shares[index].astype(jnp.float32)
        squares = jnp.sum(share * share, axis=0, keepdims=True)
        total = jnp.sum(squares, axis=1, keepdims=True)
        iterate[index] = (share * (1.0 / (jnp.sqrt(total) + grad_eps))).astype(jnp.bfloat16)

    for _ in range(NS_STEPS):
        for index in range(3):
            block = iterate[index]
            gram = contract_columns(block, block).astype(jnp.bfloat16)
            square = product(gram, gram)
            mixing = (ns_second * gram.astype(jnp.float32) + ns_third * square).astype(jnp.bfloat16)
            moved = product(mixing, block)
            iterate[index] = (ns_first * block.astype(jnp.float32) + moved).astype(jnp.bfloat16)

    fresh = []
    for index, (fast, norm, result, axis) in enumerate(
        (
            (gate, gate_norm, gate_new, 0),
            (up, up_norm, up_new, 0),
            (down, down_norm, down_new, 1),
        )
    ):
        moved = fast[...].astype(jnp.float32) - iterate[index].astype(jnp.float32)
        sums = jnp.sum(moved * moved, axis=axis, keepdims=True)
        moved = moved * (norm[...] / (jnp.sqrt(sums) + norm_eps))
        result[...] = moved.astype(jnp.bfloat16)
        fresh.append(moved.astype(jnp.bfloat16))
    gate_low, up_low, down_low = fresh
    low_queries = queries[...]
    gate_out = product(low_queries, gate_low)
    up_out = product(low_queries, up_low)
    hidden = gate_out * (0.5 + 0.5 * jnp.tanh(0.5 * gate_out)) * up_out
    output = contract_columns(hidden.astype(jnp.bfloat16), down_low)
    normed_out[...] = (rms_scale(output) * out_gain[...]).astype(jnp.bfloat16)


def trained(shares, other_shares, queries, fasts, norms, out_gain_row, active):
    width, inner = fasts[0].shape
    whole = pl.BlockSpec(memory_space=pltpu.VMEM)
    results = pl.pallas_call(
        update_kernel,
        out_shape=[
            jax.ShapeDtypeStruct(queries.shape, jnp.bfloat16),
            *(jax.ShapeDtypeStruct(fast.shape, jnp.bfloat16) for fast in fasts),
        ],
        in_specs=[pl.BlockSpec(memory_space=pltpu.SMEM)] + [whole] * 10,
        out_specs=[whole] * 4,
        scratch_shapes=[pltpu.VMEM((3, width, inner), jnp.bfloat16)],
        compiler_params=pltpu.CompilerParams(vmem_limit_bytes=30 * 2**20),
        cost_estimate=pl.CostEstimate(
            flops=12 * width * width * (2 * inner + width),
            bytes_accessed=24 * width * inner,
            transcendentals=0,
        ),
        name="update",
    )(active, shares, other_shares, queries, *fasts, *norms, out_gain_row)
    return results[0], tuple(results[1:])


def shards(stream, in_gain, w_qkv, qk_gain, w_one, w_three, w_two, token_rate, out_gain, w_out):
    segment_index = lax.axis_index("segment")
    span_count = stream.shape[0]
    qkv_matrix = w_qkv[0, :, 0].swapaxes(0, 1)
    initial = (
        w_one[0, 0],
        w_three[0, 0],
        w_two[0, 0].T,
    )
    norms = tuple(
        jnp.sqrt(jnp.sum(jnp.square(matrix.astype(jnp.float32)), axis=axis, keepdims=True))
        for matrix, axis in zip(initial, (0, 0, 1))
    )

    last = lax.axis_size("segment") - 1
    sources = [stream[span] for span in range(span_count)]
    results = None
    for segment in range(last + 1):
        active = (segment_index == segment).astype(jnp.int32)[None]

        def prepared(source, span):
            queries, own = project(
                source,
                in_gain,
                qkv_matrix,
                qk_gain[0, 0],
                token_rate[0, span][:, None],
                segment,
            )
            return (queries, *own_core_tokens(own))

        fasts, outcome, received = initial, [], []
        ready = prepared(sources[0], 0)
        for span in range(span_count):
            queries, near, far = ready
            blocks = [*near, *far]
            if span + 1 < span_count:
                following = sources[span + 1]
                *near, following = lax.optimization_barrier((*near, following))
                blocks = [*near, *far]
                ready = prepared(following, span + 1)
                held, later = lax.optimization_barrier((blocks[-1], ready[0]))
                blocks = blocks[:-1] + [held]
                ready = (later, *ready[1:])
            if received:
                held, received[-1] = lax.optimization_barrier((blocks[-1], received[-1]))
                blocks = blocks[:-1] + [held]
            shares = gradient_shares(blocks, fasts, active)
            other_shares = turned(shares, "seq_2", 1)
            if span + 1 < span_count:
                later, near, far = ready
                *near, other_shares = lax.optimization_barrier((*near, other_shares))
                ready = (later, near, far)
            normed_out, fasts = trained(
                shares, other_shares, queries, fasts, norms, out_gain[0], active
            )
            if span + 1 < span_count:
                later, near, far = ready
                *far, normed_out = lax.optimization_barrier((*far, normed_out))
                ready = (later, near, far)
            head_terms = product(normed_out, w_out[0, 0])
            delta = summed_columns(head_terms, "head")
            outcome.append((sources[span].astype(jnp.float32) + delta).astype(jnp.bfloat16))
            if segment < last:
                received.append(turned(outcome[-1], "segment", 1))
        chosen = segment_index == segment
        results = (
            outcome
            if results is None
            else [jnp.where(chosen, fresh, former) for fresh, former in zip(outcome, results)]
        )
        sources = received
    return jnp.stack(results)[None]


def solution(mesh):
    torus = Mesh(
        mesh.devices.reshape(mesh.shape["segment"], 2, 4, 2, mesh.shape["head"]),
        ("segment", "seq_0", "seq_1", "seq_2", "head"),
    )
    return jax.shard_map(
        shards,
        mesh=torus,
        in_specs=(
            P(None, SEQ, "head"),
            P("segment", None),
            P("segment", None, "head", None, None),
            P("segment", "head", None, None),
            P("segment", "head", None, None),
            P("segment", "head", None, None),
            P("segment", "head", None, None),
            P("segment", None, SEQ),
            P("segment", "head", None),
            P("segment", "head", None, None),
        ),
        out_specs=P("segment", None, SEQ, "head"),
        check_vma=False,
    )
```

```python
import functools

import jax
import jax.numpy as jnp
from jax import lax
from jax.experimental import pallas as pl
from jax.experimental.pallas import tpu as pltpu
from jax.sharding import Mesh
from jax.sharding import PartitionSpec as P

NS_STEPS = 2
SEQ = ("seq_0", "seq_1", "seq_2")

ns_first = 3.4445
ns_second = -4.775
ns_third = 2.0315
norm_eps = 1e-06
grad_eps = 1e-07
VMEM_LIMIT = 30 * 2**20
SMALL_COST = pl.CostEstimate(flops=1000, bytes_accessed=1000, transcendentals=0)


def turned(array, axis, by):
    devices = lax.axis_size(axis)
    return lax.ppermute(array, axis, [(i, (i + by) % devices) for i in range(devices)])


def others(array, axis):
    return [turned(array, axis, by) for by in range(1, lax.axis_size(axis))]


def head_columns(array, axis):
    devices = lax.axis_size(axis)
    here = lax.axis_index(axis)
    width = array.shape[1] // devices

    def piece(index):
        return lax.dynamic_slice_in_dim(array, index * width, width, 1)

    arrived = [
        turned(piece((here + by) % devices).astype(jnp.bfloat16), axis, by)
        for by in range(1, devices)
    ]
    return arrived, piece(here)


def gathered_blocks(block):
    return [block, *others(block, "head")]


def own_core_tokens(block):
    across = turned(block, "seq_0", 1)
    return across, [block, *others(block, "seq_1")], others(across, "seq_1")


def rms_scale(values):
    return values * lax.rsqrt(jnp.mean(values * values, axis=-1, keepdims=True) + norm_eps)


def contract_columns(left, right):
    return lax.dot_general(
        left, right, (((1,), (1,)), ((), ())), preferred_element_type=jnp.float32
    )


def product(left, right):
    return jnp.dot(left, right, preferred_element_type=jnp.float32)


def project_kernel(places, *refs):
    blocks = refs[:-9]
    gain, source, head_gains, rates, queries, pairs, weights, total, sems = refs[-9:]
    heads = len(blocks)
    columns = blocks[0].shape[1]
    width = queries.shape[1]
    active = places[heads] == 1

    @pl.when(active)
    def _():
        starts = [pl.multiple_of(places[index] * columns, columns) for index in range(heads)]
        copies = [
            [
                pltpu.make_async_copy(
                    source.at[third, pl.ds(start, columns)],
                    weights.at[third, index * columns : (index + 1) * columns],
                    sems.at[index, third],
                )
                for third in range(3)
            ]
            for index, start in enumerate(starts)
        ]
        for group in copies:
            for copy in group:
                copy.start()
        rows = blocks[0].shape[0]
        rate = jnp.broadcast_to(rates[...], (rows, rows)).T[:, :1]
        squares = jnp.zeros((rows, 1), jnp.float32)
        for block in blocks:
            values = block[...].astype(jnp.float32)
            squares = squares + jnp.sum(values * values, axis=1, keepdims=True)
        scale = lax.rsqrt(squares / (heads * columns) + norm_eps)
        for index, (block, start) in enumerate(zip(blocks, starts)):
            values = block[...].astype(jnp.float32)
            normed = (values * scale * gain[:, pl.ds(start, columns)]).astype(jnp.bfloat16)
            for third in range(3):
                copies[index][third].wait()
                part = slice(third * width, (third + 1) * width)
                share = product(normed, weights[third, index * columns : (index + 1) * columns])
                if index == 0:
                    total[:, part] = share
                else:
                    total[:, part] += share
        queries[...] = (rms_scale(total[:, :width]) * head_gains[0:1, :]).astype(jnp.bfloat16)
        key_rows = rms_scale(total[:, width : 2 * width]) * head_gains[1:2, :]
        pairs[:, :width] = key_rows.astype(jnp.bfloat16)
        pairs[:, width:] = (-rate * total[:, 2 * width :]).astype(jnp.bfloat16)

    @pl.when(jnp.logical_not(active))
    def _():
        queries[...] = jnp.zeros_like(queries)
        pairs[...] = jnp.zeros_like(pairs)


def project(blocks, gain_row, qkv_matrix, head_gains, rate_row, segment):
    heads = len(blocks)
    rows = blocks[0].shape[0]
    width = head_gains.shape[1]
    here = lax.axis_index("head")
    active = (lax.axis_index("segment") == segment).astype(jnp.int32)
    places = jnp.stack([(here - by) % heads for by in range(heads)] + [active])
    whole = pl.BlockSpec(memory_space=pltpu.VMEM)
    return pl.pallas_call(
        project_kernel,
        out_shape=[
            jax.ShapeDtypeStruct((rows, width), jnp.bfloat16),
            jax.ShapeDtypeStruct((rows, 2 * width), jnp.bfloat16),
        ],
        in_specs=[
            pl.BlockSpec(memory_space=pltpu.SMEM),
            *[whole] * (heads + 1),
            pl.BlockSpec(memory_space=pl.ANY),
            *[whole] * 2,
        ],
        out_specs=[whole] * 2,
        scratch_shapes=[
            pltpu.VMEM(qkv_matrix.shape, jnp.bfloat16),
            pltpu.VMEM((rows, 3 * width), jnp.float32),
            pltpu.SemaphoreType.DMA((heads, 3)),
        ],
        compiler_params=pltpu.CompilerParams(vmem_limit_bytes=56 * 2**20),
        cost_estimate=SMALL_COST,
        name="project",
    )(places, *blocks, gain_row, qkv_matrix, head_gains, rate_row)


def gradient_kernel(active, *refs):
    blocks = refs[:-10]
    fasts, sums, tokens, weights, turned_keys, turned_grads, grads, shares, sems, last_sems = refs[-10:]

    @pl.when(active[0] == 1)
    def _():
        count, width = tokens.shape[0], weights.shape[1]
        inner = weights.shape[2]
        height = blocks[0].shape[0]
        rows, columns = 512, 256
        load = pltpu.make_async_copy(fasts, weights, last_sems.at[3])
        load.start()
        copies = [
            pltpu.make_async_copy(
                block, tokens.at[index * height : (index + 1) * height], sems.at[index]
            )
            for index, block in enumerate(blocks)
        ]
        for copy in copies:
            copy.start()
        for copy in copies:
            copy.wait()
        load.wait()

        @pl.loop(0, count // rows)
        def _(step):
            lines = pl.ds(pl.multiple_of(step * rows, rows), rows)
            key_rows = tokens[lines, :width]
            out_grad = tokens[lines, width:]
            turned_keys[:, lines] = key_rows.T
            turned_grads[:, lines] = out_grad.T
            for start in range(0, inner, columns):
                part = slice(start, start + columns)
                pre_gate = product(key_rows, weights[0, :, part])
                pre_up = product(key_rows, weights[1, :, part])
                backward = product(out_grad, weights[2, :, part])
                sigmoid_gate = 0.5 + 0.5 * jnp.tanh(0.5 * pre_gate)
                gated = pre_gate * sigmoid_gate
                slope = sigmoid_gate + gated * (1.0 - sigmoid_gate)
                grads[0, lines, part] = (backward * pre_up * slope).astype(jnp.bfloat16)
                grads[1, lines, part] = (backward * gated).astype(jnp.bfloat16)
                grads[2, lines, part] = (gated * pre_up).astype(jnp.bfloat16)

        stores = [
            pltpu.make_async_copy(shares.at[index], sums.at[index], last_sems.at[index])
            for index in range(3)
        ]
        for index, left in enumerate((turned_keys, turned_keys, turned_grads)):
            for start in range(0, inner, columns):
                part = slice(start, start + columns)
                share = product(left[...], grads[index, :, part])
                shares[index, :, part] = share.astype(jnp.bfloat16)
            stores[index].start()
        for store in stores:
            store.wait()


def gradient_shares(blocks, fasts, active):
    count = blocks[0].shape[0] * len(blocks)
    _, width, inner = fasts.shape
    anywhere = pl.BlockSpec(memory_space=pl.ANY)
    return pl.pallas_call(
        gradient_kernel,
        out_shape=jax.ShapeDtypeStruct((3, width, inner), jnp.bfloat16),
        in_specs=[pl.BlockSpec(memory_space=pltpu.SMEM)] + [anywhere] * (len(blocks) + 1),
        out_specs=anywhere,
        scratch_shapes=[
            pltpu.VMEM((count, 2 * width), jnp.bfloat16),
            pltpu.VMEM((3, width, inner), jnp.bfloat16),
            pltpu.VMEM((width, count), jnp.bfloat16),
            pltpu.VMEM((width, count), jnp.bfloat16),
            pltpu.VMEM((3, count, inner), jnp.bfloat16),
            pltpu.VMEM((3, width, inner), jnp.bfloat16),
            pltpu.SemaphoreType.DMA((len(blocks),)),
            pltpu.SemaphoreType.DMA((4,)),
        ],
        compiler_params=pltpu.CompilerParams(vmem_limit_bytes=VMEM_LIMIT),
        cost_estimate=SMALL_COST,
        name="gradients",
    )(active, *blocks, fasts)


def update_kernel(active, *refs):
    normed_out = refs[6]

    @pl.when(active[0] == 1)
    def _():
        update(*refs)

    @pl.when(active[0] != 1)
    def _():
        normed_out[...] = jnp.zeros_like(normed_out)


def update(
    shares,
    other_shares,
    fasts,
    initial,
    queries,
    out_gain,
    normed_out,
    result,
    iterate,
    mine,
    theirs,
    weights,
    started,
    fasts_new,
    sems,
):
    loads = [
        pltpu.make_async_copy(source, target, sems.at[index])
        for index, (source, target) in enumerate(
            ((shares, mine), (other_shares, theirs), (fasts, weights), (initial, started))
        )
    ]
    for load in loads:
        load.start()
    loads[0].wait()
    loads[1].wait()
    for index in range(3):
        share = mine[index].astype(jnp.float32) + theirs[index].astype(jnp.float32)
        squares = jnp.sum(share * share, axis=0, keepdims=True)
        total = jnp.sum(squares, axis=1, keepdims=True)
        iterate[index] = (share * (1.0 / (jnp.sqrt(total) + grad_eps))).astype(jnp.bfloat16)

    for _ in range(NS_STEPS):
        for index in range(3):
            block = iterate[index]
            gram = contract_columns(block, block).astype(jnp.bfloat16)
            square = product(gram, gram)
            mixing = (ns_second * gram.astype(jnp.float32) + ns_third * square).astype(jnp.bfloat16)
            moved = product(mixing, block)
            iterate[index] = (ns_first * block.astype(jnp.float32) + moved).astype(jnp.bfloat16)

    loads[2].wait()
    loads[3].wait()
    stores = [
        pltpu.make_async_copy(fasts_new.at[index], result.at[index], sems.at[4 + index])
        for index in range(3)
    ]
    for index, axis in enumerate((0, 0, 1)):
        first = started[index].astype(jnp.float32)
        norm = jnp.sqrt(jnp.sum(first * first, axis=axis, keepdims=True))
        moved = weights[index].astype(jnp.float32) - iterate[index].astype(jnp.float32)
        sums = jnp.sum(moved * moved, axis=axis, keepdims=True)
        moved = moved * (norm / (jnp.sqrt(sums) + norm_eps))
        fasts_new[index] = moved.astype(jnp.bfloat16)
        stores[index].start()
    low_queries = queries[...]
    gate_out = product(low_queries, fasts_new[0])
    up_out = product(low_queries, fasts_new[1])
    hidden = gate_out * (0.5 + 0.5 * jnp.tanh(0.5 * gate_out)) * up_out
    output = contract_columns(hidden.astype(jnp.bfloat16), fasts_new[2])
    normed_out[...] = (rms_scale(output) * out_gain[...]).astype(jnp.bfloat16)
    for store in stores:
        store.wait()


def trained(shares, other_shares, fasts, initial_fasts, queries, out_gain_row, active):
    whole = pl.BlockSpec(memory_space=pltpu.VMEM)
    anywhere = pl.BlockSpec(memory_space=pl.ANY)
    _, width, inner = fasts.shape
    return pl.pallas_call(
        update_kernel,
        out_shape=[
            jax.ShapeDtypeStruct(queries.shape, jnp.bfloat16),
            jax.ShapeDtypeStruct(fasts.shape, jnp.bfloat16),
        ],
        in_specs=[pl.BlockSpec(memory_space=pltpu.SMEM)] + [anywhere] * 4 + [whole] * 2,
        out_specs=[whole, anywhere],
        scratch_shapes=[
            *[pltpu.VMEM(fasts.shape, jnp.bfloat16)] * 6,
            pltpu.SemaphoreType.DMA((7,)),
        ],
        compiler_params=pltpu.CompilerParams(vmem_limit_bytes=VMEM_LIMIT),
        cost_estimate=SMALL_COST,
        name="update",
    )(active, shares, other_shares, fasts, initial_fasts, queries, out_gain_row)


def shards(stream, in_gain, w_qkv, qk_gain, w_one, w_three, w_two, token_rate, out_gain, w_out):
    segment_index = lax.axis_index("segment")
    span_count = stream.shape[0]
    qkv_matrix = w_qkv[0, :, 0].swapaxes(0, 1)
    initial_fasts = jnp.stack([w_one[0, 0], w_three[0, 0], w_two[0, 0].T])
    gain_row, initial_fasts = lax.optimization_barrier((in_gain, initial_fasts))
    last = lax.axis_size("segment") - 1
    sources = [stream[span] for span in range(span_count)]
    results, gathered = None, None
    for segment in range(last + 1):
        active = (segment_index == segment).astype(jnp.int32)[None]

        def prepared(blocks, span):
            return project(
                blocks,
                gain_row,
                qkv_matrix,
                qk_gain[0, 0],
                token_rate[0, span][None, :],
                segment,
            )

        fasts, outcome, received = initial_fasts, [], []
        if gathered is None:
            gathered = gathered_blocks(sources[0])
        queries, own = prepared(gathered, 0)
        across, near, far = own_core_tokens(own)
        for span in range(span_count):
            follows = span + 1 < span_count
            if follows:
                following = sources[span + 1]
                if segment == 0:
                    own, following = lax.optimization_barrier((own, following))
                else:
                    far[0], far[1], following = lax.optimization_barrier(
                        (far[0], far[1], following)
                    )
                later, own = prepared(gathered_blocks(following), span + 1)
                far[-1], later = lax.optimization_barrier((far[-1], later))
                next_across, next_near, next_far = own_core_tokens(own)
            shares = gradient_shares([*near, across, *far], fasts, active)
            other_shares = turned(shares, "seq_2", 1)
            if follows:
                next_across, other_shares = lax.optimization_barrier((next_across, other_shares))
            normed_out, fasts = trained(
                shares, other_shares, fasts, initial_fasts, queries, out_gain[0], active
            )
            if follows:
                *next_near, normed_out = lax.optimization_barrier((*next_near, normed_out))
            if received:
                gathered = gathered_blocks(received[0])
                gathered[-1], normed_out = lax.optimization_barrier((gathered[-1], normed_out))
            head_terms = product(normed_out, w_out[0, 0])
            if follows:
                queries, across, near, far = later, next_across, next_near, next_far
            arrived, delta = head_columns(head_terms, "head")
            if follows and segment < last:
                tied = lax.optimization_barrier((*far, *arrived))
                far, arrived = list(tied[: len(far)]), list(tied[len(far) :])
            for part in arrived:
                delta = delta + part.astype(jnp.float32)
            outcome.append((sources[span].astype(jnp.float32) + delta).astype(jnp.bfloat16))
            if segment < last:
                received.append(lax.ppermute(outcome[-1], "segment", [(segment, segment + 1)]))
        chosen = segment_index == segment
        results = (
            outcome
            if results is None
            else [jnp.where(chosen, fresh, former) for fresh, former in zip(outcome, results)]
        )
        sources = received
    return jnp.stack(results)[None]


def solution(mesh):
    torus = Mesh(
        mesh.devices.reshape(mesh.shape["segment"], 2, 4, 2, mesh.shape["head"]),
        ("segment", "seq_0", "seq_1", "seq_2", "head"),
    )
    return jax.shard_map(
        shards,
        mesh=torus,
        in_specs=(
            P(None, SEQ, "head"),
            P("segment", None),
            P("segment", None, "head", None, None),
            P("segment", "head", None, None),
            P("segment", "head", None, None),
            P("segment", "head", None, None),
            P("segment", "head", None, None),
            P("segment", None, SEQ),
            P("segment", "head", None),
            P("segment", "head", None, None),
        ),
        out_specs=P("segment", None, SEQ, "head"),
        check_vma=False,
    )
```

```python
import functools

import jax
import jax.numpy as jnp
from jax import lax
from jax.experimental import pallas as pl
from jax.experimental.pallas import tpu as pltpu
from jax.sharding import Mesh
from jax.sharding import PartitionSpec as P

NS_STEPS = 2
SEQ = ("seq_0", "seq_1", "seq_2")

ns_first = 3.4445
ns_second = -4.775
ns_third = 2.0315
norm_eps = 1e-06
grad_eps = 1e-07
VMEM_LIMIT = 30 * 2**20
SMALL_COST = pl.CostEstimate(flops=4 * 10**9, bytes_accessed=10**7, transcendentals=0)


def turned(array, axis, by):
    devices = lax.axis_size(axis)
    return lax.ppermute(array, axis, [(i, (i + by) % devices) for i in range(devices)])


def others(array, axis):
    return [turned(array, axis, by) for by in range(1, lax.axis_size(axis))]


def head_columns(array, axis):
    devices = lax.axis_size(axis)
    here = lax.axis_index(axis)
    width = array.shape[1] // devices

    def piece(index):
        return lax.dynamic_slice_in_dim(array, index * width, width, 1)

    arrived = [
        turned(piece((here + by) % devices).astype(jnp.bfloat16), axis, by)
        for by in range(1, devices)
    ]
    return arrived, piece(here)


def gathered_blocks(block):
    return [block, *others(block, "head")]


def own_core_tokens(block):
    across = turned(block, "seq_0", 1)
    return across, [block, *others(block, "seq_1")], others(across, "seq_1")


def rms_scale(values):
    return values * lax.rsqrt(jnp.mean(values * values, axis=-1, keepdims=True) + norm_eps)


def contract_columns(left, right):
    return lax.dot_general(
        left, right, (((1,), (1,)), ((), ())), preferred_element_type=jnp.float32
    )


def product(left, right):
    return jnp.dot(left, right, preferred_element_type=jnp.float32)


def project_kernel(places, *refs):
    blocks = refs[:-9]
    gain, source, head_gains, rates, queries, pairs, weights, total, sems = refs[-9:]
    heads = len(blocks)
    columns = blocks[0].shape[1]
    width = queries.shape[1]
    active = places[heads] == 1

    @pl.when(active)
    def _():
        starts = [pl.multiple_of(places[index] * columns, columns) for index in range(heads)]
        copies = [
            [
                pltpu.make_async_copy(
                    source.at[third, pl.ds(start, columns)],
                    weights.at[third, index * columns : (index + 1) * columns],
                    sems.at[index, third],
                )
                for third in range(3)
            ]
            for index, start in enumerate(starts)
        ]
        for group in copies:
            for copy in group:
                copy.start()
        rows = blocks[0].shape[0]
        rate = jnp.broadcast_to(rates[...], (rows, rows)).T[:, :1]
        squares = jnp.zeros((rows, 1), jnp.float32)
        for block in blocks:
            values = block[...].astype(jnp.float32)
            squares = squares + jnp.sum(values * values, axis=1, keepdims=True)
        scale = lax.rsqrt(squares / (heads * columns) + norm_eps)
        for index, (block, start) in enumerate(zip(blocks, starts)):
            values = block[...].astype(jnp.float32)
            normed = (values * scale * gain[:, pl.ds(start, columns)]).astype(jnp.bfloat16)
            for third in range(3):
                copies[index][third].wait()
                part = slice(third * width, (third + 1) * width)
                share = product(normed, weights[third, index * columns : (index + 1) * columns])
                if index == 0:
                    total[:, part] = share
                else:
                    total[:, part] += share
        queries[...] = (rms_scale(total[:, :width]) * head_gains[0:1, :]).astype(jnp.bfloat16)
        key_rows = rms_scale(total[:, width : 2 * width]) * head_gains[1:2, :]
        pairs[:, :width] = key_rows.astype(jnp.bfloat16)
        pairs[:, width:] = (-rate * total[:, 2 * width :]).astype(jnp.bfloat16)

    @pl.when(jnp.logical_not(active))
    def _():
        queries[...] = jnp.zeros_like(queries)
        pairs[...] = jnp.zeros_like(pairs)


def project(blocks, gain_row, qkv_matrix, head_gains, rate_row, segment):
    heads = len(blocks)
    rows = blocks[0].shape[0]
    width = head_gains.shape[1]
    here = lax.axis_index("head")
    active = (lax.axis_index("segment") == segment).astype(jnp.int32)
    places = jnp.stack([(here - by) % heads for by in range(heads)] + [active])
    whole = pl.BlockSpec(memory_space=pltpu.VMEM)
    return pl.pallas_call(
        project_kernel,
        out_shape=[
            jax.ShapeDtypeStruct((rows, width), jnp.bfloat16),
            jax.ShapeDtypeStruct((rows, 2 * width), jnp.bfloat16),
        ],
        in_specs=[
            pl.BlockSpec(memory_space=pltpu.SMEM),
            *[whole] * (heads + 1),
            pl.BlockSpec(memory_space=pl.ANY),
            *[whole] * 2,
        ],
        out_specs=[whole] * 2,
        scratch_shapes=[
            pltpu.VMEM(qkv_matrix.shape, jnp.bfloat16),
            pltpu.VMEM((rows, 3 * width), jnp.float32),
            pltpu.SemaphoreType.DMA((heads, 3)),
        ],
        compiler_params=pltpu.CompilerParams(vmem_limit_bytes=56 * 2**20),
        cost_estimate=SMALL_COST,
        name="project",
    )(places, *blocks, gain_row, qkv_matrix, head_gains, rate_row)


def gradient_kernel(active, *refs):
    blocks = refs[:-10]
    fasts, sums, tokens, weights, turned_keys, turned_grads, grads, shares, sems, last_sems = refs[-10:]

    @pl.when(active[0] == 1)
    def _():
        count, width = tokens.shape[0], weights.shape[1]
        inner = weights.shape[2]
        height = blocks[0].shape[0]
        rows, columns = 512, 256
        load = pltpu.make_async_copy(fasts, weights, last_sems.at[3])
        load.start()
        copies = [
            pltpu.make_async_copy(
                block, tokens.at[index * height : (index + 1) * height], sems.at[index]
            )
            for index, block in enumerate(blocks)
        ]
        for copy in copies:
            copy.start()
        for copy in copies:
            copy.wait()
        load.wait()

        @pl.loop(0, count // rows)
        def _(step):
            lines = pl.ds(pl.multiple_of(step * rows, rows), rows)
            key_rows = tokens[lines, :width]
            out_grad = tokens[lines, width:]
            turned_keys[:, lines] = key_rows.T
            turned_grads[:, lines] = out_grad.T
            for start in range(0, inner, columns):
                part = slice(start, start + columns)
                pre_gate = product(key_rows, weights[0, :, part])
                pre_up = product(key_rows, weights[1, :, part])
                backward = product(out_grad, weights[2, :, part])
                sigmoid_gate = 0.5 + 0.5 * jnp.tanh(0.5 * pre_gate)
                gated = pre_gate * sigmoid_gate
                slope = sigmoid_gate + gated * (1.0 - sigmoid_gate)
                grads[0, lines, part] = (backward * pre_up * slope).astype(jnp.bfloat16)
                grads[1, lines, part] = (backward * gated).astype(jnp.bfloat16)
                grads[2, lines, part] = (gated * pre_up).astype(jnp.bfloat16)

        stores = [
            pltpu.make_async_copy(shares.at[index], sums.at[index], last_sems.at[index])
            for index in range(3)
        ]
        for index, left in enumerate((turned_keys, turned_keys, turned_grads)):
            for start in range(0, inner, columns):
                part = slice(start, start + columns)
                share = product(left[...], grads[index, :, part])
                shares[index, :, part] = share.astype(jnp.bfloat16)
            stores[index].start()
        for store in stores:
            store.wait()


def gradient_shares(blocks, fasts, active):
    count = blocks[0].shape[0] * len(blocks)
    _, width, inner = fasts.shape
    anywhere = pl.BlockSpec(memory_space=pl.ANY)
    return pl.pallas_call(
        gradient_kernel,
        out_shape=jax.ShapeDtypeStruct((3, width, inner), jnp.bfloat16),
        in_specs=[pl.BlockSpec(memory_space=pltpu.SMEM)] + [anywhere] * (len(blocks) + 1),
        out_specs=anywhere,
        scratch_shapes=[
            pltpu.VMEM((count, 2 * width), jnp.bfloat16),
            pltpu.VMEM((3, width, inner), jnp.bfloat16),
            pltpu.VMEM((width, count), jnp.bfloat16),
            pltpu.VMEM((width, count), jnp.bfloat16),
            pltpu.VMEM((3, count, inner), jnp.bfloat16),
            pltpu.VMEM((3, width, inner), jnp.bfloat16),
            pltpu.SemaphoreType.DMA((len(blocks),)),
            pltpu.SemaphoreType.DMA((4,)),
        ],
        compiler_params=pltpu.CompilerParams(vmem_limit_bytes=VMEM_LIMIT),
        cost_estimate=SMALL_COST,
        name="gradients",
    )(active, *blocks, fasts)


def update_kernel(active, *refs):
    normed_out = refs[6]

    @pl.when(active[0] == 1)
    def _():
        update(*refs)

    @pl.when(active[0] != 1)
    def _():
        normed_out[...] = jnp.zeros_like(normed_out)


def update(
    shares,
    other_shares,
    fasts,
    initial,
    queries,
    out_gain,
    normed_out,
    result,
    iterate,
    mine,
    theirs,
    weights,
    started,
    fasts_new,
    sems,
):
    loads = [
        pltpu.make_async_copy(source, target, sems.at[index])
        for index, (source, target) in enumerate(
            ((shares, mine), (other_shares, theirs), (fasts, weights), (initial, started))
        )
    ]
    for load in loads:
        load.start()
    loads[0].wait()
    loads[1].wait()
    for index in range(3):
        share = mine[index].astype(jnp.float32) + theirs[index].astype(jnp.float32)
        squares = jnp.sum(share * share, axis=0, keepdims=True)
        total = jnp.sum(squares, axis=1, keepdims=True)
        iterate[index] = (share * (1.0 / (jnp.sqrt(total) + grad_eps))).astype(jnp.bfloat16)

    for _ in range(NS_STEPS):
        for index in range(3):
            block = iterate[index]
            gram = contract_columns(block, block).astype(jnp.bfloat16)
            square = product(gram, gram)
            mixing = (ns_second * gram.astype(jnp.float32) + ns_third * square).astype(jnp.bfloat16)
            moved = product(mixing, block)
            iterate[index] = (ns_first * block.astype(jnp.float32) + moved).astype(jnp.bfloat16)

    loads[2].wait()
    loads[3].wait()
    stores = [
        pltpu.make_async_copy(fasts_new.at[index], result.at[index], sems.at[4 + index])
        for index in range(3)
    ]
    for index, axis in enumerate((0, 0, 1)):
        first = started[index].astype(jnp.float32)
        norm = jnp.sqrt(jnp.sum(first * first, axis=axis, keepdims=True))
        moved = weights[index].astype(jnp.float32) - iterate[index].astype(jnp.float32)
        sums = jnp.sum(moved * moved, axis=axis, keepdims=True)
        moved = moved * (norm / (jnp.sqrt(sums) + norm_eps))
        fasts_new[index] = moved.astype(jnp.bfloat16)
        stores[index].start()
    low_queries = queries[...]
    gate_out = product(low_queries, fasts_new[0])
    up_out = product(low_queries, fasts_new[1])
    hidden = gate_out * (0.5 + 0.5 * jnp.tanh(0.5 * gate_out)) * up_out
    output = contract_columns(hidden.astype(jnp.bfloat16), fasts_new[2])
    normed_out[...] = (rms_scale(output) * out_gain[...]).astype(jnp.bfloat16)
    for store in stores:
        store.wait()


def trained(shares, other_shares, fasts, initial_fasts, queries, out_gain_row, active):
    whole = pl.BlockSpec(memory_space=pltpu.VMEM)
    anywhere = pl.BlockSpec(memory_space=pl.ANY)
    _, width, inner = fasts.shape
    return pl.pallas_call(
        update_kernel,
        out_shape=[
            jax.ShapeDtypeStruct(queries.shape, jnp.bfloat16),
            jax.ShapeDtypeStruct(fasts.shape, jnp.bfloat16),
        ],
        in_specs=[pl.BlockSpec(memory_space=pltpu.SMEM)] + [anywhere] * 4 + [whole] * 2,
        out_specs=[whole, anywhere],
        scratch_shapes=[
            *[pltpu.VMEM(fasts.shape, jnp.bfloat16)] * 6,
            pltpu.SemaphoreType.DMA((7,)),
        ],
        compiler_params=pltpu.CompilerParams(vmem_limit_bytes=VMEM_LIMIT),
        cost_estimate=SMALL_COST,
        name="update",
    )(active, shares, other_shares, fasts, initial_fasts, queries, out_gain_row)


def shards(stream, in_gain, w_qkv, qk_gain, w_one, w_three, w_two, token_rate, out_gain, w_out):
    segment_index = lax.axis_index("segment")
    span_count = stream.shape[0]
    qkv_matrix = w_qkv[0, :, 0].swapaxes(0, 1)
    initial_fasts = jnp.stack([w_one[0, 0], w_three[0, 0], w_two[0, 0].T])
    gain_row, initial_fasts = lax.optimization_barrier((in_gain, initial_fasts))
    last = lax.axis_size("segment") - 1
    sources = [stream[span] for span in range(span_count)]
    results, gathered = None, None
    for segment in range(last + 1):
        active = (segment_index == segment).astype(jnp.int32)[None]

        def prepared(blocks, span):
            return project(
                blocks,
                gain_row,
                qkv_matrix,
                qk_gain[0, 0],
                token_rate[0, span][None, :],
                segment,
            )

        fasts, outcome, received = initial_fasts, [], []
        if gathered is None:
            gathered = gathered_blocks(sources[0])
        queries, own = prepared(gathered, 0)
        across, near, far = own_core_tokens(own)
        for span in range(span_count):
            follows = span + 1 < span_count
            if follows:
                following = sources[span + 1]
                if segment == 0:
                    own, following = lax.optimization_barrier((own, following))
                else:
                    far[0], far[1], following = lax.optimization_barrier(
                        (far[0], far[1], following)
                    )
                later, own = prepared(gathered_blocks(following), span + 1)
                far[-1], later = lax.optimization_barrier((far[-1], later))
                next_across, next_near, next_far = own_core_tokens(own)
            shares = gradient_shares([*near, across, *far], fasts, active)
            other_shares = turned(shares, "seq_2", 1)
            if follows:
                next_across, other_shares = lax.optimization_barrier((next_across, other_shares))
            normed_out, fasts = trained(
                shares, other_shares, fasts, initial_fasts, queries, out_gain[0], active
            )
            if follows:
                *next_near, normed_out = lax.optimization_barrier((*next_near, normed_out))
            if received:
                gathered = gathered_blocks(received[0])
                gathered[-1], normed_out = lax.optimization_barrier((gathered[-1], normed_out))
            head_terms = product(normed_out, w_out[0, 0])
            if follows:
                queries, across, near, far = later, next_across, next_near, next_far
            arrived, delta = head_columns(head_terms, "head")
            if follows and segment < last:
                tied = lax.optimization_barrier((*far, *arrived))
                far, arrived = list(tied[: len(far)]), list(tied[len(far) :])
            for part in arrived:
                delta = delta + part.astype(jnp.float32)
            outcome.append((sources[span].astype(jnp.float32) + delta).astype(jnp.bfloat16))
            if segment < last:
                received.append(lax.ppermute(outcome[-1], "segment", [(segment, segment + 1)]))
        chosen = segment_index == segment
        results = (
            outcome
            if results is None
            else [jnp.where(chosen, fresh, former) for fresh, former in zip(outcome, results)]
        )
        sources = received
    return jnp.stack(results)[None]


def solution(mesh):
    torus = Mesh(
        mesh.devices.reshape(mesh.shape["segment"], 2, 4, 2, mesh.shape["head"]),
        ("segment", "seq_0", "seq_1", "seq_2", "head"),
    )
    return jax.shard_map(
        shards,
        mesh=torus,
        in_specs=(
            P(None, SEQ, "head"),
            P("segment", None),
            P("segment", None, "head", None, None),
            P("segment", "head", None, None),
            P("segment", "head", None, None),
            P("segment", "head", None, None),
            P("segment", "head", None, None),
            P("segment", None, SEQ),
            P("segment", "head", None),
            P("segment", "head", None, None),
        ),
        out_specs=P("segment", None, SEQ, "head"),
        check_vma=False,
    )
```
